32 devices in a mesh: group: 2 (over x), tensor: 16 (over z, y, core).
Axes of the slice: x: 2, y: 2, z: 4, core: 2. Of those that a mesh axis runs over, the one named last changes fastest.
Arguments:
- residual_input: bfloat16 [32, 8192], P('group', 'tensor'), parts along dimension 0, may hold values from -40 to 40
- attention_norm_gain: bfloat16 [8192], replicated, may hold values from 0.3984375 to 2.5
- query_weight: bfloat16 [8192, 8192], P(None, 'tensor'), may hold values from -0.0625 to 0.0625
- key_value_weight: bfloat16 [8192, 2048], P(None, 'tensor'), may hold values from -0.0625 to 0.0625
- output_weight: bfloat16 [8192, 8192], P('tensor'), may hold values from -0.09375 to 0.09375
- adapter_down_weight: bfloat16 [16, 8192, 192], P('group', 'tensor'), parts along dimension 0, may hold values from -0.0625 to 0.0625
- adapter_up_query: bfloat16 [16, 64, 8192], P('group', None, 'tensor'), parts along dimension 0, may hold values from -0.75 to 0.75
- adapter_up_key_value: bfloat16 [16, 64, 2048], P('group', None, 'tensor'), parts along dimension 0, may hold values from -0.75 to 0.75
- stored_key_cache: bfloat16 [32, 512, 1024], P(('group', 'tensor')), parts along dimension 0, may hold values from -250 to 250
- stored_value_cache: bfloat16 [32, 512, 1024], P(('group', 'tensor')), parts along dimension 0, may hold values from -8 to 8
- row_adapter_index: int32 [32], P('group'), parts along dimension 0, may hold values from 0 to 7
- cache_live_length: int32 [32], P(('group', 'tensor')), parts along dimension 0, may hold values from 2 to 508, as said below
Outputs:
- hidden_out: bfloat16 [32, 8192], P('group', 'tensor'), parts along dimension 0
- new_keyval: bfloat16 [32, 4, 2048], P(('group', 'tensor')), parts along dimension 0
The draws below stay inside these ranges and needn't reach their ends.
There are 2 independent parts, one for each index of `group`. The reference program is written for one: setup_inputs(seed, part) draws one part's arguments, and reference() takes and returns one part's arrays. A program takes and returns all parts, laid end to end along the dimension named above; an argument that names none is the same for every part. Nothing has to cross between parts.
Inputs may be any that keep to these rules, and one draw needn't show every extreme that they name: `cache_live_length`: some row's length is exactly 508, so every new key fits the cache.
All inputs are finite; a program needn't handle non-finite values.
Results may differ from the reference program's by a relative error of at most 0.029.
The reference program's roundings to bfloat16 on the way count: a program that leaves them out, or rounds other values in their place, can miss the bound.
Values may be sent and summed in bfloat16 or wider, within the bound.
A program may use at most 128 MiB of HBM per device.

```python
import math
import jax
import jax.numpy as jnp
import numpy as np
from jax import lax

MODEL_WIDTH = 8192
QUERY_HEADS = 64
KEY_VALUE_HEADS = 8
HEAD_SIZE = 128
ADAPTER_RANK = 64
ADAPTER_COUNT = 8
CACHE_CAPACITY = 512
DECODE_STEPS = 4
REPLICA_ROWS = 16


def draw_residual_input(key, part):
    key = jax.random.fold_in(key, 11)
    initial_random_key, another_random_key, third_key = jax.random.split(key, 3)
    row_scale = jnp.exp(jax.random.uniform(initial_random_key, (REPLICA_ROWS, 1), minval=0.0, maxval=jnp.log(10.0)))
    column_scale = jnp.exp(jax.random.uniform(another_random_key, (1, MODEL_WIDTH), minval=0.0, maxval=jnp.log(10.0)))
    base_projection = jnp.clip(jax.random.normal(third_key, (REPLICA_ROWS, MODEL_WIDTH)), -4.0, 4.0)
    return (0.1 * base_projection * row_scale * column_scale).astype(jnp.bfloat16)


def draw_stored_key_cache(key, part):
    key = jax.random.fold_in(key, 37)
    initial_random_key = jax.random.fold_in(key, 0)
    sampled_keys = jnp.clip(jax.random.normal(initial_random_key, (REPLICA_ROWS, CACHE_CAPACITY, KEY_VALUE_HEADS * HEAD_SIZE)), -4.0, 4.0)
    return sampled_keys.astype(jnp.bfloat16)


def draw_cache_live_length(key, part):
    key = jax.random.fold_in(key, 23)
    initial_random_key, another_random_key, third_key = jax.random.split(key, 3)
    longest = CACHE_CAPACITY - DECODE_STEPS
    first_draw = jax.random.randint(initial_random_key, (REPLICA_ROWS,), 0, longest - 1)
    second_draw = jax.random.randint(another_random_key, (REPLICA_ROWS,), 0, longest - 1)
    lengths = 2 + first_draw * second_draw // (longest - 2)
    chosen = jax.random.randint(third_key, (), 0, REPLICA_ROWS)
    lengths = jnp.where(jnp.arange(REPLICA_ROWS) == chosen, longest, lengths)
    return jnp.minimum(lengths, longest).astype(jnp.int32)


def plant(array, own_key, low, high):
    spot = [jax.random.randint(jax.random.fold_in(own_key, axis), (), 0, length) for axis, length in enumerate(array.shape)]
    widest = array.shape.index(max(array.shape))
    beside = spot[:widest] + [(spot[widest] + 1) % array.shape[widest]] + spot[widest + 1:]
    return array.at[tuple(spot)].set(low).at[tuple(beside)].set(high)


def raised(values, own_key, source, target, blocks, factor):
    owner, partner = [(jnp.arange(values.shape[dim]) // (values.shape[dim] // blocks)).reshape([-1 if axis == dim else 1 for axis in range(values.ndim)]) for dim in (source, target)]
    chosen = jax.random.permutation(own_key, blocks)[partner]
    strong = (owner == chosen) | (owner == (partner + blocks // 2) % blocks)
    return jnp.where(strong, factor * values, values)


def level_of(own_key, shape, cuts, low, high):
    gain = 1.0
    for dim, blocks in cuts:
        steps = jax.random.uniform(jax.random.fold_in(jax.random.fold_in(own_key, 6), dim), (blocks,), jnp.float32, low / len(cuts), high / len(cuts))
        gain = gain * jnp.repeat(jnp.exp(steps), shape[dim] // blocks).reshape((-1,) + (1,) * (len(shape) - 1 - dim))
    return gain


def rank_table(amount, lean):
    weights = [(1 << 20) // math.isqrt(rank ** lean) + 1 for rank in range(1, amount + 1)]
    spread = 1 + sum(weights) // (1 << 30)
    return np.cumsum(np.array([max(1, weight // spread) for weight in weights]))


def ranked(rng, shape, number_of, slope):
    grid = rank_table(number_of, slope)
    lot = jax.random.randint(jax.random.fold_in(rng, 1), shape, 0, int(grid[number_of - 1]))
    rank = jnp.searchsorted(jnp.asarray(grid, jnp.int32), lot, side="right")
    return jax.random.permutation(jax.random.fold_in(rng, 2), number_of)[rank].astype(jnp.int32)


def gaussian(own_key, shape, spread, bound, shards=(), kind=jnp.bfloat16):
    factor_of = level_of(own_key, shape, shards, -0.22, 0.18) if shards else 1.0
    drawn = jax.random.normal(own_key, shape, jnp.float32) * spread * factor_of
    return jnp.minimum(jnp.maximum(drawn, -bound), bound).astype(kind)


def heavy_noise(own_key, extent, width, reach, pieces, heavy, held_as=jnp.bfloat16):
    entries = width * jax.random.normal(own_key, extent, jnp.float32)
    if pieces:
        entries = entries * level_of(own_key, extent, pieces, -0.22, 0.18)
    return jnp.clip(raised(entries, jax.random.fold_in(own_key, 3), *heavy), -reach, reach).astype(held_as)


def setup_inputs(seed: int = 0, part: int = 0) -> dict:
    streams_of = jax.random.split(jax.random.key(seed), 13)
    part_keys = jax.random.split(jax.random.fold_in(streams_of[12], part), 13)
    return {
        "residual_input": draw_residual_input(jax.random.fold_in(jax.random.fold_in(streams_of[12], part), 71), part),
        "attention_norm_gain": jnp.clip(jnp.exp(jax.random.uniform(streams_of[1], (MODEL_WIDTH,), jnp.float32, math.log(0.3984375), math.log(2.5))), 0.3984375, 2.5).astype(jnp.bfloat16),
        "query_weight": gaussian(streams_of[2], (MODEL_WIDTH, QUERY_HEADS * HEAD_SIZE), MODEL_WIDTH ** -0.5, 0.0625, ((1, 16),)),
        "key_value_weight": gaussian(streams_of[3], (MODEL_WIDTH, 2 * KEY_VALUE_HEADS * HEAD_SIZE), MODEL_WIDTH ** -0.5, 0.0625, ((1, 16),)),
        "output_weight": heavy_noise(streams_of[4], (QUERY_HEADS * HEAD_SIZE, MODEL_WIDTH), (QUERY_HEADS * HEAD_SIZE) ** -0.5, 0.09375, ((0, 16),), (0, 1, 16, 2.0)),
        "adapter_down_weight": gaussian(part_keys[5], (ADAPTER_COUNT, MODEL_WIDTH, 3 * ADAPTER_RANK), MODEL_WIDTH ** -0.5, 0.0625, ((1, 16),)),
        "adapter_up_query": gaussian(part_keys[6], (ADAPTER_COUNT, ADAPTER_RANK, QUERY_HEADS * HEAD_SIZE), ADAPTER_RANK ** -0.5, 0.75, ((2, 16),)),
        "adapter_up_key_value": gaussian(part_keys[7], (ADAPTER_COUNT, ADAPTER_RANK, 2 * KEY_VALUE_HEADS * HEAD_SIZE), ADAPTER_RANK ** -0.5, 0.75, ((2, 16),)),
        "stored_key_cache": draw_stored_key_cache(jax.random.fold_in(jax.random.fold_in(streams_of[12], part), 71), part),
        "stored_value_cache": gaussian(part_keys[9], (REPLICA_ROWS, CACHE_CAPACITY, KEY_VALUE_HEADS * HEAD_SIZE), 2.0, 8.0, ((0, 16),)),
        "row_adapter_index": plant(ranked(part_keys[10], (REPLICA_ROWS,), ADAPTER_COUNT, 2), jax.random.fold_in(part_keys[10], 3), 0, ADAPTER_COUNT - 1).astype(jnp.int32),
        "cache_live_length": draw_cache_live_length(jax.random.fold_in(jax.random.fold_in(streams_of[12], part), 71), part),
    }


eps = 1e-05
rope_base = 500000.0
adapter_scale = 0.5

def apply_rotary(values_in, token_positions):
    halfway = HEAD_SIZE // 2
    frequency = rope_base ** (-jnp.arange(halfway, dtype=jnp.float32) / halfway)
    angles = token_positions.astype(jnp.float32)[:, None] * frequency[None, :]
    cosine = jnp.cos(angles)[:, None, :]
    sine_part = jnp.sin(angles)[:, None, :]
    first_half = values_in[..., :halfway]
    second_half = values_in[..., halfway:]
    return jnp.concatenate([first_half * cosine - second_half * sine_part, second_half * cosine + first_half * sine_part], axis=-1)

def rms_norm(hidden_state, gain_vec):
    widened = hidden_state.astype(jnp.float32)
    mean_sq = lax.optimization_barrier(jnp.mean(widened * widened, axis=1, keepdims=True))
    return (widened * lax.rsqrt(mean_sq + eps) * gain_vec.astype(jnp.float32)[None, :]).astype(jnp.bfloat16)

def adapter_partial(adapter_onehot_mask, inputs, weights):
    accumulated = jnp.zeros((inputs.shape[0], weights.shape[2]), jnp.float32)
    for adapter in range(ADAPTER_COUNT):
        accumulated = accumulated + adapter_onehot_mask[:, adapter:adapter + 1] * jnp.dot(inputs, weights[adapter], preferred_element_type=jnp.float32)
    return accumulated

def reference(residual_input, attention_norm_gain, query_weight, key_value_weight, output_weight, adapter_down_weight, adapter_up_query, adapter_up_key_value, stored_key_cache, stored_value_cache, row_adapter_index, cache_live_length):
    total_row_count = residual_input.shape[0]
    query_group_count = QUERY_HEADS // KEY_VALUE_HEADS
    key_value_width = KEY_VALUE_HEADS * HEAD_SIZE
    adapter_onehot_mask = (row_adapter_index[:, None] == jnp.arange(ADAPTER_COUNT, dtype=jnp.int32)[None, :]).astype(jnp.float32)
    previous_keys = stored_key_cache.astype(jnp.float32).reshape(total_row_count, CACHE_CAPACITY, KEY_VALUE_HEADS, HEAD_SIZE)
    previous_values = stored_value_cache.astype(jnp.float32).reshape(total_row_count, CACHE_CAPACITY, KEY_VALUE_HEADS, HEAD_SIZE)
    live_mask = jnp.arange(CACHE_CAPACITY, dtype=jnp.int32)[None, :] < cache_live_length[:, None]
    newest_keys = jnp.zeros((total_row_count, DECODE_STEPS, KEY_VALUE_HEADS, HEAD_SIZE), jnp.float32)
    newest_values = jnp.zeros((total_row_count, DECODE_STEPS, KEY_VALUE_HEADS, HEAD_SIZE), jnp.float32)
    hidden_state = residual_input
    for single_decode_pass in range(DECODE_STEPS):
        normalized_input = rms_norm(hidden_state, attention_norm_gain)
        reduced_features = adapter_partial(adapter_onehot_mask, normalized_input, adapter_down_weight).astype(jnp.bfloat16)
        query_projected = jnp.dot(normalized_input, query_weight, preferred_element_type=jnp.float32) + adapter_scale * adapter_partial(adapter_onehot_mask, reduced_features[:, :ADAPTER_RANK], adapter_up_query)
        adapter_key_delta = adapter_partial(adapter_onehot_mask, reduced_features[:, ADAPTER_RANK:2 * ADAPTER_RANK], adapter_up_key_value[:, :, :key_value_width])
        adapter_value_delta = adapter_partial(adapter_onehot_mask, reduced_features[:, 2 * ADAPTER_RANK:], adapter_up_key_value[:, :, key_value_width:])
        key_value_proj = jnp.dot(normalized_input, key_value_weight, preferred_element_type=jnp.float32) + adapter_scale * jnp.concatenate([adapter_key_delta, adapter_value_delta], axis=1)
        query_projected = query_projected.astype(jnp.bfloat16)
        key_value_proj = key_value_proj.astype(jnp.bfloat16)
        token_positions = cache_live_length + single_decode_pass
        rotated_query_rows = apply_rotary(query_projected.astype(jnp.float32).reshape(total_row_count, QUERY_HEADS, HEAD_SIZE), token_positions).astype(jnp.bfloat16)
        rotated_key_rows = apply_rotary(key_value_proj[:, :key_value_width].astype(jnp.float32).reshape(total_row_count, KEY_VALUE_HEADS, HEAD_SIZE), token_positions).astype(jnp.bfloat16)
        newest_keys = newest_keys.at[:, single_decode_pass].set(rotated_key_rows.astype(jnp.float32))
        newest_values = newest_values.at[:, single_decode_pass].set(key_value_proj[:, key_value_width:].astype(jnp.float32).reshape(total_row_count, KEY_VALUE_HEADS, HEAD_SIZE))
        grouped_query = rotated_query_rows.astype(jnp.float32).reshape(total_row_count, KEY_VALUE_HEADS, query_group_count, HEAD_SIZE)
        old_scores = jnp.einsum('rkgd,rjkd->rkgj', grouped_query, previous_keys) * HEAD_SIZE ** (-0.5)
        old_scores = jnp.where(live_mask[:, None, None, :], old_scores, -jnp.inf)
        new_scores = jnp.einsum('rkgd,rmkd->rkgm', grouped_query, newest_keys) * HEAD_SIZE ** (-0.5)
        visible = jnp.arange(DECODE_STEPS, dtype=jnp.int32)[None, None, None, :] <= single_decode_pass
        new_scores = jnp.where(visible, new_scores, -jnp.inf)
        row_top = jnp.maximum(lax.optimization_barrier(jnp.max(old_scores, axis=3, keepdims=True)), lax.optimization_barrier(jnp.max(new_scores, axis=3, keepdims=True)))
        old_exp = jnp.exp(old_scores - row_top)
        new_exp = jnp.exp(new_scores - row_top)
        denominator = lax.optimization_barrier(jnp.sum(old_exp, axis=3, keepdims=True)) + lax.optimization_barrier(jnp.sum(new_exp, axis=3, keepdims=True))
        old_weights = (old_exp / denominator).astype(jnp.bfloat16).astype(jnp.float32)
        new_weights = (new_exp / denominator).astype(jnp.bfloat16).astype(jnp.float32)
        mixture = jnp.einsum('rkgj,rjkd->rkgd', old_weights, previous_values) + jnp.einsum('rkgm,rmkd->rkgd', new_weights, newest_values)
        attended = mixture.astype(jnp.bfloat16).reshape(total_row_count, QUERY_HEADS * HEAD_SIZE)
        hidden_state = (hidden_state.astype(jnp.float32) + jnp.dot(attended, output_weight, preferred_element_type=jnp.float32)).astype(jnp.bfloat16)
    new_keyval = jnp.concatenate([newest_keys.reshape(total_row_count, DECODE_STEPS, key_value_width), newest_values.reshape(total_row_count, DECODE_STEPS, key_value_width)], axis=2).astype(jnp.bfloat16)
    return (hidden_state, new_keyval)
```

```python
import functools

import jax
import jax.numpy as jnp
from jax import lax
from jax.experimental import pallas as pl
from jax.experimental.pallas import tpu as pltpu
from jax.sharding import PartitionSpec as P

QUERY_HEADS = 64
KEY_VALUE_HEADS = 8
HEAD_SIZE = 128
ADAPTER_RANK = 64
ADAPTER_COUNT = 8
BLK = 16
CACHE_CAPACITY = 512
DECODE_STEPS = 4


eps = 1e-05
rope_base = 500000.0
adapter_scale = 0.5
MESH = pl.DeviceIdType.MESH
F32 = jnp.float32
BF16 = jnp.bfloat16
WEIGHT_PIECES = 4
PADDED_HEADS = 8
PARTIAL_TYPE = jnp.float32


def apply_rotary(values_in, token_positions):
    halfway = HEAD_SIZE // 2
    frequency = rope_base ** (-jnp.arange(halfway, dtype=jnp.float32) / halfway)
    angles = token_positions.astype(jnp.float32)[:, None] * frequency[None, :]
    cosine = jnp.cos(angles)[:, None, :]
    sine_part = jnp.sin(angles)[:, None, :]
    first_half = values_in[..., :halfway]
    second_half = values_in[..., halfway:]
    return jnp.concatenate(
        [
            first_half * cosine - second_half * sine_part,
            second_half * cosine + first_half * sine_part,
        ],
        axis=-1,
    )


def rms_norm(hidden_state, gain_vec):
    widened = hidden_state.astype(jnp.float32)
    mean_sq = jnp.mean(widened * widened, axis=1, keepdims=True)
    return (widened * lax.rsqrt(mean_sq + eps) * gain_vec.astype(jnp.float32)[None, :]).astype(
        jnp.bfloat16
    )


def block_tables(row_adapter_index):
    total_row_count = row_adapter_index.shape[0]
    nblocks = total_row_count // BLK + ADAPTER_COUNT
    onehot = (
        row_adapter_index[:, None] == jnp.arange(ADAPTER_COUNT, dtype=jnp.int32)[None, :]
    ).astype(jnp.int32)
    counts = jnp.sum(onehot, axis=0)
    adapter_partial = (counts + BLK - 1) // BLK
    first_block = jnp.cumsum(adapter_partial) - adapter_partial
    earlier = jnp.cumsum(onehot, axis=0) - onehot
    rank_in = jnp.sum(onehot * earlier, axis=1)
    start_block = jnp.sum(onehot * first_block[None, :], axis=1)
    slot_of_row = (start_block + rank_in // BLK) * BLK + rank_in % BLK
    slots = jnp.arange(nblocks * BLK, dtype=jnp.int32)
    matches = (slot_of_row[None, :] == slots[:, None]).astype(jnp.int32)
    filled = jnp.sum(matches, axis=1)
    row_of_slot = jnp.sum(matches * jnp.arange(total_row_count, dtype=jnp.int32)[None, :], axis=1)
    blocks = jnp.arange(nblocks, dtype=jnp.int32)
    block_end = first_block + adapter_partial
    owner = jnp.minimum(
        jnp.sum((block_end[None, :] <= blocks[:, None]).astype(jnp.int32), axis=1),
        ADAPTER_COUNT - 1,
    )
    return (slot_of_row, row_of_slot, filled, owner)


def split_into_blocks(inputs, weights, page_tables):
    slot_of_row, row_of_slot, filled, owner = page_tables
    nblocks = owner.shape[0]
    gathered = jnp.take(inputs, row_of_slot, axis=0) * filled[:, None].astype(inputs.dtype)
    gathered = gathered.reshape(nblocks, BLK, inputs.shape[1])
    chosen = jnp.take(weights, owner, axis=0)
    products = jnp.einsum("bsk,bkm->bsm", gathered, chosen, preferred_element_type=jnp.float32)
    return jnp.take(products.reshape(nblocks * BLK, weights.shape[2]), slot_of_row, axis=0)


def attend(
    query_projected,
    key_value_proj,
    stored_key_cache,
    stored_value_cache,
    cache_live_length,
    newest_keys,
    newest_values,
    single_decode_pass,
):
    moved_query, shifted_key_value = (
        lax.all_to_all(query_projected, "tensor", split_axis=0, concat_axis=1, tiled=True),
        lax.all_to_all(key_value_proj, "tensor", split_axis=0, concat_axis=1, tiled=True),
    )
    replica_local_count = moved_query.shape[0]
    query_group_count = QUERY_HEADS // KEY_VALUE_HEADS
    key_value_width = KEY_VALUE_HEADS * HEAD_SIZE
    token_positions = cache_live_length + single_decode_pass
    rotated_query_rows = apply_rotary(
        moved_query.astype(jnp.float32).reshape(replica_local_count, QUERY_HEADS, HEAD_SIZE),
        token_positions,
    ).astype(jnp.bfloat16)
    rotated_key_rows = apply_rotary(
        shifted_key_value[:, :key_value_width]
        .astype(jnp.float32)
        .reshape(replica_local_count, KEY_VALUE_HEADS, HEAD_SIZE),
        token_positions,
    ).astype(jnp.bfloat16)
    newest_keys = newest_keys.at[:, single_decode_pass].set(rotated_key_rows)
    newest_values = newest_values.at[:, single_decode_pass].set(
        shifted_key_value[:, key_value_width:].reshape(
            replica_local_count, KEY_VALUE_HEADS, HEAD_SIZE
        )
    )
    grouped_query = rotated_query_rows.reshape(
        replica_local_count, KEY_VALUE_HEADS, query_group_count, HEAD_SIZE
    )
    previous_keys = stored_key_cache.reshape(
        replica_local_count, CACHE_CAPACITY, KEY_VALUE_HEADS, HEAD_SIZE
    )
    previous_values = stored_value_cache.reshape(
        replica_local_count, CACHE_CAPACITY, KEY_VALUE_HEADS, HEAD_SIZE
    )
    old_scores = jnp.einsum(
        "rkgd,rjkd->rkgj", grouped_query, previous_keys, preferred_element_type=jnp.float32
    ) * HEAD_SIZE ** (-0.5)
    live_mask = jnp.arange(CACHE_CAPACITY, dtype=jnp.int32)[None, :] < cache_live_length[:, None]
    old_scores = jnp.where(live_mask[:, None, None, :], old_scores, -jnp.inf)
    new_scores = jnp.einsum(
        "rkgd,rmkd->rkgm", grouped_query, newest_keys, preferred_element_type=jnp.float32
    ) * HEAD_SIZE ** (-0.5)
    visible = jnp.arange(DECODE_STEPS, dtype=jnp.int32)[None, None, None, :] <= single_decode_pass
    new_scores = jnp.where(visible, new_scores, -jnp.inf)
    row_top = jnp.maximum(
        jnp.max(old_scores, axis=3, keepdims=True), jnp.max(new_scores, axis=3, keepdims=True)
    )
    old_exp = jnp.exp(old_scores - row_top)
    new_exp = jnp.exp(new_scores - row_top)
    denominator = jnp.sum(old_exp, axis=3, keepdims=True) + jnp.sum(new_exp, axis=3, keepdims=True)
    old_weights = (old_exp / denominator).astype(jnp.bfloat16)
    new_weights = (new_exp / denominator).astype(jnp.bfloat16)
    mixture = jnp.einsum(
        "rkgj,rjkd->rkgd", old_weights, previous_values, preferred_element_type=jnp.float32
    )
    mixture = mixture + jnp.einsum(
        "rkgm,rmkd->rkgd", new_weights, newest_values, preferred_element_type=jnp.float32
    )
    attended_rows = mixture.astype(jnp.bfloat16).reshape(
        replica_local_count, QUERY_HEADS * HEAD_SIZE
    )
    return (attended_rows, newest_keys, newest_values)


def body(
    residual_input,
    attention_norm_gain,
    query_weight,
    key_value_weight,
    output_weight,
    adapter_down_weight,
    adapter_up_query,
    adapter_up_key_value,
    stored_key_cache,
    stored_value_cache,
    row_adapter_index,
    cache_live_length,
):
    devices_along = lax.axis_size("tensor")
    position_in = lax.axis_index("tensor")
    share_width = residual_input.shape[1]
    replica_local_count = stored_key_cache.shape[0]
    key_value_width = KEY_VALUE_HEADS * HEAD_SIZE
    page_tables = block_tables(row_adapter_index)
    newest_keys = jnp.zeros(
        (replica_local_count, DECODE_STEPS, KEY_VALUE_HEADS, HEAD_SIZE), jnp.bfloat16
    )
    newest_values = jnp.zeros(
        (replica_local_count, DECODE_STEPS, KEY_VALUE_HEADS, HEAD_SIZE), jnp.bfloat16
    )
    hidden_state = residual_input
    for single_decode_pass in range(DECODE_STEPS):
        gathered = lax.all_gather(hidden_state, "tensor", axis=1, tiled=True)
        normalized_input = rms_norm(gathered, attention_norm_gain)
        normalized_portion = lax.dynamic_slice_in_dim(
            normalized_input, position_in * share_width, share_width, 1
        )
        reduced_features = lax.psum(
            split_into_blocks(normalized_portion, adapter_down_weight, page_tables), "tensor"
        ).astype(jnp.bfloat16)
        query_projected = jnp.dot(
            normalized_input, query_weight, preferred_element_type=jnp.float32
        )
        query_projected = query_projected + adapter_scale * split_into_blocks(
            reduced_features[:, :ADAPTER_RANK], adapter_up_query, page_tables
        )
        selected_rank = jnp.where(
            position_in < devices_along // 2,
            reduced_features[:, ADAPTER_RANK : 2 * ADAPTER_RANK],
            reduced_features[:, 2 * ADAPTER_RANK :],
        )
        key_value_proj = jnp.dot(
            normalized_input, key_value_weight, preferred_element_type=jnp.float32
        )
        key_value_proj = key_value_proj + adapter_scale * split_into_blocks(
            selected_rank, adapter_up_key_value, page_tables
        )
        attended_rows, newest_keys, newest_values = attend(
            query_projected.astype(jnp.bfloat16),
            key_value_proj.astype(jnp.bfloat16),
            stored_key_cache,
            stored_value_cache,
            cache_live_length,
            newest_keys,
            newest_values,
            single_decode_pass,
        )
        attended = lax.all_to_all(attended_rows, "tensor", split_axis=1, concat_axis=0, tiled=True)
        out_term = jnp.dot(attended, output_weight, preferred_element_type=jnp.float32)
        summed = lax.psum_scatter(out_term, "tensor", scatter_dimension=1, tiled=True)
        hidden_state = (hidden_state.astype(jnp.float32) + summed).astype(jnp.bfloat16)
    new_keyval = jnp.concatenate(
        [
            newest_keys.reshape(replica_local_count, DECODE_STEPS, key_value_width),
            newest_values.reshape(replica_local_count, DECODE_STEPS, key_value_width),
        ],
        axis=2,
    )
    return (hidden_state, new_keyval)


def dot(a, b):
    return jnp.dot(a, b, preferred_element_type=F32)


def decode_kernel(
    n,
    residual,
    gain,
    row_adapter,
    cosine,
    sine,
    bias,
    wq_hbm,
    wkv_hbm,
    wo_hbm,
    down_hbm,
    upq_hbm,
    upkv_hbm,
    kc_hbm,
    vc_hbm,
    hidden_out,
    keyval_out,
    wq,
    wkv,
    wo,
    down,
    upq,
    upkv,
    kc,
    vc,
    hidden,
    gathered,
    normed,
    dn_send,
    dn_recv,
    qkv_send,
    qkv_recv,
    att_send,
    att_recv,
    pair_send,
    pair_recv,
    chip_send,
    chip_recv,
    kept,
    wq_sem,
    wkv_sem,
    load_sem,
    ag_send_sem,
    ag_fwd_sem,
    ag_recv_sem,
    dn_send_sem,
    dn_recv_sem,
    qkv_send_sem,
    qkv_recv_sem,
    att_send_sem,
    att_recv_sem,
    pair_send_sem,
    pair_recv_sem,
    chip_send_sem,
    chip_recv_sem,
):
    rows, width = residual.shape
    model = n * width
    head = HEAD_SIZE
    query_blocks = width // head
    chips = n // 2
    me = lax.axis_index("tensor")
    core = lax.rem(me, 2)
    chip = lax.div(me, 2)
    partner = me + 1 - 2 * core
    piece = model // WEIGHT_PIECES

    def wq_load(i):
        part = pl.ds(i * piece, piece)
        return pltpu.make_async_copy(wq_hbm.at[part], wq.at[part], wq_sem.at[i])

    def wkv_load(i):
        part = pl.ds(i * piece, piece)
        return pltpu.make_async_copy(wkv_hbm.at[part], wkv.at[part], wkv_sem.at[i])

    def load(source, target, i):
        return pltpu.make_async_copy(source, target, load_sem.at[i])

    down_load = load(down_hbm, down, 0)
    upq_load = load(upq_hbm, upq, 1)
    upkv_load = load(upkv_hbm, upkv, 2)
    kc_load = load(kc_hbm, kc, 3)
    vc_load = load(vc_hbm, vc, 4)
    wo_load = load(wo_hbm, wo, 5)

    down_load.start()
    for i in range(WEIGHT_PIECES):
        wq_load(i).start()
        wkv_load(i).start()
    for copy in (upq_load, upkv_load, kc_load, vc_load, wo_load):
        copy.start()

    def loop(low, high, action):
        def step(k, carry):
            action(k)
            return carry

        lax.fori_loop(low, high, step, 0)

    barrier = pltpu.get_barrier_semaphore()

    def greet(k):
        pl.semaphore_signal(
            barrier, inc=1, device_id={"tensor": lax.rem(me + k, n)}, device_id_type=MESH
        )

    loop(1, n, greet)

    hidden[...] = residual[...]
    qkv_send[...] = jnp.zeros_like(qkv_send)
    pl.semaphore_wait(barrier, n - 1)

    def remote(source, target, send, recv, device):
        return pltpu.make_async_remote_copy(
            src_ref=source,
            dst_ref=target,
            send_sem=send,
            recv_sem=recv,
            device_id={"tensor": device},
            device_id_type=MESH,
        )

    def chip_after(k):
        return lax.rem(chip + k, chips)

    def chip_before(k):
        return lax.rem(chip + chips - k, chips)

    def ag_direct(k):
        return remote(
            hidden,
            gathered.at[me],
            ag_send_sem.at[k],
            ag_recv_sem.at[me],
            2 * chip_after(k) + core,
        )

    def ag_pair():
        return remote(hidden, gathered.at[me], ag_send_sem.at[0], ag_recv_sem.at[me], partner)

    def ag_arrival(source):
        return remote(
            hidden, gathered.at[source], ag_send_sem.at[0], ag_recv_sem.at[source], partner
        )

    def ag_forward(k):
        source = 2 * chip_before(k) + core
        return remote(
            gathered.at[source],
            gathered.at[source],
            ag_fwd_sem.at[k],
            ag_recv_sem.at[source],
            partner,
        )

    def exchange(send, recv, send_sem, recv_sem, unit):
        def block(ref, i):
            return ref.at[pl.ds(pl.multiple_of(i * unit, unit), unit)]

        def outgoing(k):
            target = lax.rem(me + k, n)
            return remote(
                block(send, target), block(recv, me), send_sem.at[k], recv_sem.at[me], target
            )

        def incoming(k):
            source = lax.rem(me + n - k, n)
            return remote(
                block(send, source), block(recv, source), send_sem.at[k], recv_sem.at[source], source
            )

        def start():
            loop(1, n, lambda k: outgoing(k).start())
            own = pl.ds(pl.multiple_of(me * unit, unit), unit)
            recv[own, :] = send[own, :]

        def finish():
            loop(1, n, lambda k: incoming(k).wait_recv())
            loop(1, n, lambda k: outgoing(k).wait_send())

        return start, finish

    qkv_start, qkv_finish = exchange(qkv_send, qkv_recv, qkv_send_sem, qkv_recv_sem, PADDED_HEADS)
    att_start, att_finish = exchange(att_send, att_recv, att_send_sem, att_recv_sem, PADDED_HEADS)

    def dn_out(k):
        target = lax.rem(me + k, n)
        half = lax.div(target, n // 2)
        return remote(
            dn_send.at[half], dn_recv.at[me], dn_send_sem.at[k], dn_recv_sem.at[me], target
        )

    def dn_in(k):
        source = lax.rem(me + n - k, n)
        return remote(
            dn_send.at[0], dn_recv.at[source], dn_send_sem.at[k], dn_recv_sem.at[source], source
        )

    def pair_copy(j):
        return remote(
            pair_send.at[j], pair_recv.at[j], pair_send_sem.at[j], pair_recv_sem.at[j], partner
        )

    def chip_copy(j):
        return remote(
            chip_send.at[j],
            chip_recv.at[j],
            chip_send_sem.at[j],
            chip_recv_sem.at[j],
            2 * chip_after(j + 1) + core,
        )

    adapter = row_adapter[...]

    def spread(values):
        twice = jnp.concatenate([values, values], axis=1)
        lane = lax.broadcasted_iota(jnp.int32, twice.shape, 1)
        second = (lane >= ADAPTER_RANK).astype(jnp.int32)
        parts = [
            jnp.where(adapter == second + 2 * j, twice, jnp.zeros_like(twice))
            for j in range(ADAPTER_COUNT // 2)
        ]
        return jnp.concatenate(parts, axis=1).astype(BF16)

    def decode_step(t):
        first = t == 0
        loop(1, chips, lambda k: ag_direct(k).start())
        ag_pair().start()
        gathered[me] = hidden[...]

        def pass_on(k):
            ag_arrival(2 * chip_before(k) + core).wait_recv()
            ag_forward(k).start()

        loop(1, chips, pass_on)
        loop(0, chips, lambda k: ag_arrival(2 * chip_before(k) + 1 - core).wait_recv())

        total = jnp.zeros((rows, width), F32)
        for k in range(n):
            block = gathered[k].astype(F32)
            total = total + block * block
        scale = lax.rsqrt(jnp.sum(total, axis=1, keepdims=True) * (1.0 / model) + eps)

        mine = pl.ds(pl.multiple_of(me * width, width), width)
        own = (hidden[...].astype(F32) * scale * gain[:, mine]).astype(BF16)

        @pl.when(first)
        def _():
            down_load.wait()

        partial = jnp.zeros((rows, down.shape[2]), F32)
        for a in range(ADAPTER_COUNT):
            partial = partial + jnp.where(adapter == a, dot(own, down[a]), 0.0)
        for_query = partial[:, :ADAPTER_RANK]
        dn_send[0] = partial[:, : 2 * ADAPTER_RANK]
        dn_send[1] = jnp.concatenate([for_query, partial[:, 2 * ADAPTER_RANK :]], axis=1)
        loop(1, n, lambda k: dn_out(k).start())
        dn_recv[me] = dn_send[lax.div(me, n // 2)]

        for k in range(n):
            block = gathered[k].astype(F32)
            here = slice(k * width, (k + 1) * width)
            normed[:, here] = (block * scale * gain[:, here]).astype(BF16)

        query = jnp.zeros((rows, width), F32)
        keyval = jnp.zeros((rows, wkv.shape[1]), F32)
        for i in range(WEIGHT_PIECES):

            @pl.when(first)
            def _():
                wq_load(i).wait()
                wkv_load(i).wait()

            here = slice(i * piece, (i + 1) * piece)
            part = normed[:, here]
            query = query + dot(part, wq[here, :])
            keyval = keyval + dot(part, wkv[here, :])

        @pl.when(first)
        def _():
            upq_load.wait()
            upkv_load.wait()

        loop(1, n, lambda k: dn_in(k).wait_recv())
        shrunk = dn_recv[0]
        for k in range(1, n):
            shrunk = shrunk + dn_recv[k]
        shrunk = shrunk.astype(BF16).astype(F32)
        query = query + adapter_scale * dot(spread(shrunk[:, :ADAPTER_RANK]), upq[...])
        keyval = keyval + adapter_scale * dot(spread(shrunk[:, ADAPTER_RANK:]), upkv[...])
        query = query.astype(BF16).astype(F32)
        for h in range(query_blocks):
            qkv_send[pl.ds(h, rows, stride=PADDED_HEADS), :] = query[:, h * head : (h + 1) * head]
        qkv_send[pl.ds(query_blocks, rows, stride=PADDED_HEADS), :] = keyval.astype(BF16).astype(F32)
        qkv_start()
        loop(1, n, lambda k: dn_out(k).wait_send())
        loop(1, chips, lambda k: ag_direct(k).wait_send())
        loop(1, chips, lambda k: ag_forward(k).wait_send())
        ag_pair().wait_send()

        @pl.when(first)
        def _():
            kc_load.wait()
            vc_load.wait()

        qkv_finish()

        raw = qkv_recv[...]
        cos_row = cosine[pl.ds(t, 1), :]
        sin_row = sine[pl.ds(t, 1), :]
        rotated = raw * cos_row + pltpu.roll(raw, head // 2, 1) * sin_row
        bias_row = bias[pl.ds(t, 1), :]
        capacity = kc.shape[0]
        tail = slice(capacity - 16, capacity)
        sub = lax.broadcasted_iota(jnp.int32, (16, head), 0)
        fresh = sub == 16 - DECODE_STEPS + t
        for g in range(KEY_VALUE_HEADS):
            here = slice(g * head, (g + 1) * head)
            at_key = PADDED_HEADS * g + query_blocks
            at_value = PADDED_HEADS * (n // 2 + g) + query_blocks
            new_key = rotated[at_key : at_key + 1, :]
            new_value = raw[at_value : at_value + 1, :]
            kc[tail, here] = jnp.where(fresh, new_key, kc[tail, here].astype(F32)).astype(BF16)
            vc[tail, here] = jnp.where(fresh, new_value, vc[tail, here].astype(F32)).astype(BF16)
        for g in range(KEY_VALUE_HEADS):
            here = slice(g * head, (g + 1) * head)
            heads = slice(2 * PADDED_HEADS * g, 2 * PADDED_HEADS * (g + 1))
            scores = lax.dot_general(
                rotated[heads, :].astype(BF16),
                kc[:, here],
                (((1,), (1,)), ((), ())),
                preferred_element_type=F32,
            )
            scores = scores * head ** (-0.5) + bias_row
            top = jnp.max(scores, axis=1, keepdims=True)
            powers = jnp.exp(scores - top)
            weights = powers / jnp.sum(powers, axis=1, keepdims=True)
            att_send[heads, :] = dot(weights.astype(BF16), vc[:, here]).astype(BF16).astype(F32)
        att_start()

        @pl.when(first)
        def _():
            wo_load.wait()

        att_finish()
        attended = jnp.concatenate(
            [att_recv[pl.ds(h, rows, stride=PADDED_HEADS), :] for h in range(query_blocks)], axis=1
        ).astype(BF16)

        def product(device):
            return dot(attended, wo[:, pl.ds(pl.multiple_of(device * width, width), width)])

        for j in range(chips):
            pair_send[j] = product(2 * chip_after(j + 1) + 1 - core)
            pair_copy(j).start()
        for j in range(chips):
            part = product(2 * chip_after(j + 1) + core)
            pair_copy(j).wait_recv()
            part = part + pair_recv[j]
            if j < chips - 1:
                chip_send[j] = part.astype(chip_send.dtype)
                chip_copy(j).start()
            else:
                kept[...] = part
        summed = kept[...]
        for j in range(chips - 1):
            chip_copy(j).wait_recv()
            summed = summed + chip_recv[j].astype(F32)
        hidden[...] = (hidden[...].astype(F32) + summed).astype(BF16)
        loop(0, chips, lambda j: pair_copy(j).wait_send())
        loop(0, chips - 1, lambda j: chip_copy(j).wait_send())

    loop(0, DECODE_STEPS, decode_step)
    hidden_out[...] = hidden[...]
    end = kc.shape[0]
    keys = kc[end - 16 : end, :].astype(F32)
    values = vc[end - 16 : end, :].astype(F32)
    both = jnp.concatenate([keys, values], axis=1)
    keyval_out[...] = both[16 - DECODE_STEPS :, :].astype(BF16)


def fused_body(
    residual_input,
    attention_norm_gain,
    query_weight,
    key_value_weight,
    output_weight,
    adapter_down_weight,
    adapter_up_query,
    adapter_up_key_value,
    stored_key_cache,
    stored_value_cache,
    row_adapter_index,
    cache_live_length,
):
    n = lax.axis_size("tensor")
    rows, width = residual_input.shape
    model, kv_cols = key_value_weight.shape
    chips = n // 2
    steps = jnp.arange(DECODE_STEPS, dtype=jnp.int32)
    positions = cache_live_length[0] + steps
    halfway = HEAD_SIZE // 2
    frequency = rope_base ** (-jnp.arange(halfway, dtype=F32) / halfway)
    angles = positions.astype(F32)[:, None] * frequency[None, :]
    cosine = jnp.cos(angles)
    sine = jnp.sin(angles)
    cosine = jnp.concatenate([cosine, cosine], axis=1)
    sine = jnp.concatenate([-sine, sine], axis=1)
    capacity = stored_key_cache.shape[1]
    slots = jnp.arange(capacity, dtype=jnp.int32)
    newest = capacity - DECODE_STEPS
    live = (slots[None, :] < jnp.minimum(cache_live_length, newest)[:, None]) | (
        (slots[None, :] >= newest) & (slots[None, :] <= newest + steps[:, None])
    )
    bias = jnp.where(live, 0.0, -jnp.inf).astype(F32)
    rank_rows = ADAPTER_COUNT * ADAPTER_RANK
    vmem = pl.BlockSpec(memory_space=pltpu.VMEM)
    hbm = pl.BlockSpec(memory_space=pl.ANY)
    dma = pltpu.SemaphoreType.DMA
    key_width = stored_key_cache.shape[2]
    hidden_out, keyval_out = pl.pallas_call(
        functools.partial(decode_kernel, n),
        out_shape=(
            jax.ShapeDtypeStruct((rows, width), BF16),
            jax.ShapeDtypeStruct((DECODE_STEPS, 2 * key_width), BF16),
        ),
        in_specs=[vmem] * 6 + [hbm] * 8,
        out_specs=(vmem, vmem),
        scratch_shapes=[
            pltpu.VMEM(query_weight.shape, BF16),
            pltpu.VMEM(key_value_weight.shape, BF16),
            pltpu.VMEM(output_weight.shape, BF16),
            pltpu.VMEM(adapter_down_weight.shape, BF16),
            pltpu.VMEM((rank_rows, width), BF16),
            pltpu.VMEM((rank_rows, kv_cols), BF16),
            pltpu.VMEM((capacity, key_width), BF16),
            pltpu.VMEM((capacity, key_width), BF16),
            pltpu.VMEM((rows, width), BF16),
            pltpu.VMEM((n, rows, width), BF16),
            pltpu.VMEM((rows, model), BF16),
            pltpu.VMEM((2, rows, 2 * ADAPTER_RANK), F32),
            pltpu.VMEM((n, rows, 2 * ADAPTER_RANK), F32),
            pltpu.VMEM((n * PADDED_HEADS, HEAD_SIZE), F32),
            pltpu.VMEM((n * PADDED_HEADS, HEAD_SIZE), F32),
            pltpu.VMEM((n * PADDED_HEADS, HEAD_SIZE), F32),
            pltpu.VMEM((n * PADDED_HEADS, HEAD_SIZE), F32),
            pltpu.VMEM((chips, rows, width), F32),
            pltpu.VMEM((chips, rows, width), F32),
            pltpu.VMEM((chips - 1, rows, width), PARTIAL_TYPE),
            pltpu.VMEM((chips - 1, rows, width), PARTIAL_TYPE),
            pltpu.VMEM((rows, width), F32),
            dma((WEIGHT_PIECES,)),
            dma((WEIGHT_PIECES,)),
            dma((6,)),
            dma((chips,)),
            dma((chips,)),
            dma((n,)),
            dma((n,)),
            dma((n,)),
            dma((n,)),
            dma((n,)),
            dma((n,)),
            dma((n,)),
            dma((chips,)),
            dma((chips,)),
            dma((chips - 1,)),
            dma((chips - 1,)),
        ],
        compiler_params=pltpu.CompilerParams(
            collective_id=0, has_side_effects=True, vmem_limit_bytes=56 * 1024 * 1024
        ),
    )(
        residual_input,
        attention_norm_gain.astype(F32).reshape(1, model),
        row_adapter_index.reshape(rows, 1),
        cosine,
        sine,
        bias,
        query_weight,
        key_value_weight,
        output_weight,
        adapter_down_weight,
        adapter_up_query.reshape(rank_rows, width),
        adapter_up_key_value.reshape(rank_rows, kv_cols),
        stored_key_cache.reshape(capacity, key_width),
        stored_value_cache.reshape(capacity, key_width),
    )
    return (hidden_out, keyval_out[None])


def fits_fused(mesh):
    return mesh.shape["tensor"] == 2 * KEY_VALUE_HEADS


def solution(mesh):
    in_specs = (
        P("group", "tensor"),
        P(),
        P(None, "tensor"),
        P(None, "tensor"),
        P("tensor", None),
        P("group", "tensor", None),
        P("group", None, "tensor"),
        P("group", None, "tensor"),
        P(("group", "tensor"), None, None),
        P(("group", "tensor"), None, None),
        P("group"),
        P(("group", "tensor")),
    )
    out_specs = (P("group", "tensor"), P(("group", "tensor"), None, None))
    run = fused_body if fits_fused(mesh) else body
    return jax.shard_map(run, mesh=mesh, in_specs=in_specs, out_specs=out_specs, check_vma=False)
```
